32 devices in a mesh: gz: 4 (over y, core), wa: 8 (over z, x).
Axes of the slice: x: 2, y: 2, z: 4, core: 2. Of those that a mesh axis runs over, the one named last changes fastest.
Arguments:
- positions: float32 [3, 32768], P(None, ('gz', 'wa')), may hold values from -1.5 to 1.5
- forces: float32 [3, 32768], P(None, ('gz', 'wa')), may hold values from -6 to 6
- order: int32 [32768], P(('gz', 'wa')), may hold values from 0 to 1023, as said below
- pair_list: int32 [1792, 2], P('gz'), may hold values from 0 to 63, as said below
- pair_worker: int32 [1792], P('gz'), may hold values from 0 to 8, as said below
Outputs:
- velocities: float32 [3, 32768], P(None, ('gz', 'wa'))
The draws below stay inside these ranges and needn't reach their ends.
Inputs may be any that keep to these rules, and one draw needn't show every extreme that they name: `order`: each device's 1024 entries are a permutation of 0 to 1023. `pair_list`: in each layer's 448 rows column 0 is a block of that layer (index within the layer) and column 1 a block of that layer, or 32 plus the index of a block of the layer above; no unordered pair of blocks is listed twice in a layer; every block of a layer is paired with itself once. `pair_worker`: within one layer no worker is named by more than 56 rows, and in some layer every worker is named by exactly 56; rows of the top layer whose column 1 is 32 or more are marked 8.
All inputs are finite; a program needn't handle non-finite values.
Results may differ from the reference program's by a relative error of at most 0.00014.
Values sent between devices are 32-bit elements; how exact they have to be, the bound alone decides.
A program may use at most 64 MiB of HBM per device.

```python
import math
import jax
import jax.numpy as jnp
from jax import lax

BS = 256
BLK_DEV = 4
SLAB = 32
PAIR_GRP = 448
PDEV = 1024
NPART = 32768
PAIRS = 1792
N_GZ = 4
N_WA = 8


def candidate_pairs():
    block = jnp.arange(SLAB, dtype=jnp.int32)
    row = block // N_WA
    column = block % N_WA
    moves = [(0, 0, 0), (0, 1, 0), (1, -1, 0), (1, 0, 0), (1, 1, 0)]
    moves = moves + [(dr, dc, 1) for dr in (-1, 0, 1) for dc in (-1, 0, 1)]
    partners = [(row + dr) % BLK_DEV * N_WA + (column + dc) % N_WA + upper * SLAB for dr, dc, upper in moves]
    second = jnp.stack(partners, axis=1).reshape(-1).astype(jnp.int32)
    first = jnp.repeat(block, 14).astype(jnp.int32)
    kind = jnp.tile(jnp.arange(14, dtype=jnp.int32), SLAB)
    return (first, second, kind)


def layer_pairs(key):
    first, second, kind = candidate_pairs()
    lists = []
    workers = []
    for layer in range(N_GZ):
        sub = jax.random.fold_in(key, layer)
        key_keep, key_order, key_slot = jax.random.split(sub, 3)
        limit = 100 * (N_GZ - 1) // (N_GZ - 1 + 4 * layer)
        keep = (jax.random.randint(key_keep, (PAIR_GRP,), 0, 100) < limit) | (kind == 0)
        keep = keep & ((kind < 5) | (layer < N_GZ - 1))
        arrange = jax.random.permutation(key_order, PAIR_GRP).astype(jnp.int32)
        slots = jax.random.permutation(key_slot, PAIR_GRP).astype(jnp.int32)
        lists.append(jnp.stack([first[arrange], second[arrange]], axis=1))
        workers.append(jnp.where(keep[arrange], slots % N_WA, N_WA).astype(jnp.int32))
    return (jnp.concatenate(lists, axis=0), jnp.concatenate(workers, axis=0))


def draw_order(key, part):
    key = jax.random.fold_in(key, 11)
    devices = NPART // PDEV
    keys = jax.random.split(key, devices)
    perms = jax.vmap(lambda one: jax.random.permutation(one, PDEV))(keys)
    return perms.reshape(-1).astype(jnp.int32)


def draw_pair_list(key, part):
    lists, workers = layer_pairs(key)
    return lists


def draw_pair_worker(key, part):
    lists, workers = layer_pairs(key)
    return workers


def block_levels(stream_key, dims, pieces, smallest, top_value):
    gain = 1.0
    for axis_at, shards_of in pieces:
        draws = jax.random.uniform(jax.random.fold_in(jax.random.fold_in(stream_key, 6), axis_at), (shards_of,), jnp.float32, smallest / len(pieces), top_value / len(pieces))
        gain = gain * jnp.repeat(jnp.exp(draws), dims[axis_at] // shards_of).reshape((-1,) + (1,) * (len(dims) - 1 - axis_at))
    return gain


def bell_draw(stream_key, shape, scale, most, cuts=(), kind=jnp.bfloat16):
    factor_of = block_levels(stream_key, shape, cuts, -0.22, 0.18) if cuts else 1.0
    entries = jax.random.normal(stream_key, shape, jnp.float32) * scale * factor_of
    return jnp.minimum(jnp.maximum(entries, -most), most).astype(kind)


def setup_inputs(seed: int = 0) -> dict:
    seeds = jax.random.split(jax.random.key(seed), 6)
    positions = jnp.clip(jax.random.uniform(seeds[0], (3, NPART), jnp.float32, -1.5, 1.5) * block_levels(seeds[0], (3, NPART), ((1, 32),), -0.4, 0.0), -1.5, 1.5)
    forces = bell_draw(seeds[1], (3, NPART), 1.0, 6.0, ((1, 32),), jnp.float32)
    order = draw_order(jax.random.fold_in(seeds[5], 71), 0)
    pair_list = draw_pair_list(jax.random.fold_in(seeds[5], 71), 0)
    pair_worker = draw_pair_worker(jax.random.fold_in(seeds[5], 71), 0)
    return {"positions": positions, "forces": forces, "order": order, "pair_list": pair_list, "pair_worker": pair_worker}


radius = 0.25
screening = 1.0
prefactor = 1.0 / (4.0 * math.pi)

def tile_terms(coords_a, loads_a, coords_b, loads_b):
    highest = lax.Precision.HIGHEST
    offset = coords_a[:, :, :, None] - coords_b[:, :, None, :]
    squared = lax.optimization_barrier(jnp.sum(offset * offset, axis=1)) + radius * radius
    distance = jnp.sqrt(squared)
    screen = jax.scipy.special.erfc(screening * distance)
    gaussian = screening / math.sqrt(math.pi) * jnp.exp(-screening * screening * squared)
    isotropic = screen / distance * (0.75 + 0.5 * radius * radius / squared) + 0.5 * gaussian
    dyadic = screen / (distance * squared) * (0.75 - 1.5 * radius * radius / squared) + 0.5 * gaussian / squared
    project_b = jnp.einsum('kcij,kcj->kij', offset, loads_b, precision=highest)
    project_a = jnp.einsum('kcij,kci->kij', offset, loads_a, precision=highest)
    result_a = jnp.einsum('kij,kcj->kci', isotropic, loads_b, precision=highest) + jnp.einsum('kcij,kij->kci', offset, dyadic * project_b, precision=highest)
    result_b = jnp.einsum('kij,kci->kcj', isotropic, loads_a, precision=highest) + jnp.einsum('kcij,kij->kcj', offset, dyadic * project_a, precision=highest)
    return (prefactor * result_a, prefactor * result_b)

def reference(positions, forces, order, pair_list, pair_worker):
    count = positions.shape[1]
    per_dev = BLK_DEV * BS
    nblocks = count // BS
    source = jnp.arange(count, dtype=jnp.int32) // per_dev * per_dev + order.astype(jnp.int32)
    coords = positions[:, source].reshape(3, nblocks, BS).transpose(1, 0, 2)
    loads = forces[:, source].reshape(3, nblocks, BS).transpose(1, 0, 2)
    layer_base = jnp.arange(PAIRS, dtype=jnp.int32) // PAIR_GRP * SLAB
    first = layer_base + pair_list[:, 0]
    second = jnp.minimum(layer_base + pair_list[:, 1], nblocks - 1)
    active = (pair_worker < N_WA).astype(jnp.float32)
    twice = active * (first != second).astype(jnp.float32)
    batch = 64
    items = (first.reshape(-1, batch), second.reshape(-1, batch), active.reshape(-1, batch), twice.reshape(-1, batch))

    def step(total, item):
        first_ids, second_ids, weight_a, weight_b = item
        result_a, result_b = tile_terms(coords[first_ids], loads[first_ids], coords[second_ids], loads[second_ids])
        total = total.at[first_ids].add(weight_a[:, None, None] * result_a)
        total = total.at[second_ids].add(weight_b[:, None, None] * result_b)
        return (total, None)
    total, _ = lax.scan(step, jnp.zeros((nblocks, 3, BS), jnp.float32), items)
    blocked = total.transpose(1, 0, 2).reshape(3, count)
    return jnp.zeros((3, count), jnp.float32).at[:, source].set(blocked)
```

```python
import functools
import math

import jax
import jax.numpy as jnp
from jax import lax
from jax.experimental import pallas as pl
from jax.experimental.pallas import tpu as pltpu
from jax.sharding import PartitionSpec as P

BS = 256
ROWS = 8
CHUNK = 32

radius = 0.25
prefactor = 1.0 / (4.0 * math.pi)
half_gauss = 0.5 / math.sqrt(math.pi)
MESH = pl.DeviceIdType.MESH
F32 = jnp.float32
BF16 = jnp.bfloat16

ERFC = (0.565205955, 1.09670851, 2.38765618, -0.0810194158, 14.3292365, -25.4472659, 12.7559653)


def split2(value):
    high = value.astype(BF16)
    return high, (value - high.astype(F32)).astype(BF16)


def split3(value):
    high = value.astype(BF16)
    rest = value - high.astype(F32)
    mid = rest.astype(BF16)
    return high, mid, (rest - mid.astype(F32)).astype(BF16)


def dot(a, b, ca, cb):
    return lax.dot_general(a, b, (((ca,), (cb,)), ((), ())), preferred_element_type=F32)


def pick_kernel(pos_ref, force_ref, order_ref, out_ref):
    per_dev = pos_ref.shape[1]
    pad = jnp.zeros((2, per_dev), F32)
    parts = jnp.concatenate([pos_ref[...], force_ref[...], pad], axis=0)
    parts = jnp.concatenate([p.astype(F32) for p in split3(parts)], axis=0).astype(BF16)
    source = lax.broadcasted_iota(jnp.int32, (per_dev, BS), 0)
    for block in range(per_dev // BS):
        wanted = order_ref[:, block * BS : (block + 1) * BS]
        hot = jnp.where(source == wanted, 1.0, 0.0).astype(BF16)
        got = dot(parts, hot, 1, 0)
        out_ref[block] = (got[0:ROWS] + got[ROWS : 2 * ROWS]) + got[2 * ROWS : 3 * ROWS]


def put_kernel(value_ref, order_ref, out_ref):
    per_dev = out_ref.shape[1]
    nblocks = per_dev // BS
    source = lax.broadcasted_iota(jnp.int32, (per_dev, BS), 0)
    total = None
    for block in range(nblocks):
        value = value_ref[block * ROWS : (block + 1) * ROWS]
        parts = jnp.concatenate([p.astype(F32) for p in split3(value)], axis=0).astype(BF16)
        wanted = order_ref[:, block * BS : (block + 1) * BS]
        hot = jnp.where(source == wanted, 1.0, 0.0).astype(BF16)
        got = dot(parts, hot, 1, 1)
        total = got if total is None else total + got
    total = (total[0:ROWS] + total[ROWS : 2 * ROWS]) + total[2 * ROWS : 3 * ROWS]
    out_ref[...] = total[:3]


def spread_kernel(ngz, nwa, nblocks, mine_ref, out_ref, local_sem, send_sem, recv_sem):
    gz, wa = lax.axis_index("gz"), lax.axis_index("wa")
    lower, upper = gz > 0, gz < ngz - 1
    barrier = pltpu.get_barrier_semaphore()
    for k in range(1, nwa):
        pl.semaphore_signal(barrier, inc=1, device_id=(gz, lax.rem(wa + k, nwa)), device_id_type=MESH)

    @pl.when(upper)
    def _():
        for k in range(nwa):
            pl.semaphore_signal(barrier, inc=1, device_id=(gz + 1, lax.rem(wa + k, nwa)), device_id_type=MESH)

    own = pltpu.make_async_copy(mine_ref, out_ref.at[pl.ds(wa * nblocks, nblocks)], local_sem)
    own.start()
    pl.semaphore_wait(barrier, nwa - 1 + jnp.where(lower, nwa, 0))

    def copy(slot, to_gz, k, base):
        return pltpu.make_async_remote_copy(
            src_ref=mine_ref,
            dst_ref=out_ref.at[pl.ds(slot * nblocks, nblocks)],
            send_sem=send_sem.at[base + k],
            recv_sem=recv_sem.at[slot],
            device_id=(to_gz, lax.rem(wa + k, nwa)),
            device_id_type=MESH,
        )

    @pl.when(lower)
    def _():
        for k in range(nwa):
            copy(nwa + wa, gz - 1, k, nwa).start()

    for k in range(1, nwa):
        copy(wa, gz, k, 0).start()
    own.wait()
    for k in range(1, nwa):
        copy(lax.rem(wa + k, nwa), gz, k, 0).wait_recv()

    @pl.when(upper)
    def _():
        for k in range(nwa):
            copy(nwa + k, gz + 1, k, nwa).wait_recv()

    @pl.when(jnp.logical_not(upper))
    def _():
        out_ref[nwa * nblocks :] = jnp.zeros((nwa * nblocks, ROWS, BS), F32)

    for k in range(1, nwa):
        copy(wa, gz, k, 0).wait_send()

    @pl.when(lower)
    def _():
        for k in range(nwa):
            copy(nwa + wa, gz - 1, k, nwa).wait_send()


def collect_kernel(ngz, nwa, part_ref, out_ref, slots, send_sem, recv_sem):
    gz, wa = lax.axis_index("gz"), lax.axis_index("wa")
    lower, upper = gz > 0, gz < ngz - 1
    barrier = pltpu.get_barrier_semaphore()
    for k in range(1, nwa):
        pl.semaphore_signal(barrier, inc=1, device_id=(gz, lax.rem(wa + k, nwa)), device_id_type=MESH)

    @pl.when(lower)
    def _():
        for k in range(nwa):
            pl.semaphore_signal(barrier, inc=1, device_id=(gz - 1, lax.rem(wa + k, nwa)), device_id_type=MESH)

    pl.semaphore_wait(barrier, nwa - 1 + jnp.where(upper, nwa, 0))

    def copy(slot, to_gz, k, base):
        to = lax.rem(wa + k, nwa)
        return pltpu.make_async_remote_copy(
            src_ref=part_ref.at[base + to],
            dst_ref=slots.at[slot],
            send_sem=send_sem.at[base + k],
            recv_sem=recv_sem.at[slot],
            device_id=(to_gz, to),
            device_id_type=MESH,
        )

    @pl.when(upper)
    def _():
        for k in range(nwa):
            copy(nwa + wa, gz + 1, k, nwa).start()

    for k in range(1, nwa):
        copy(wa, gz, k, 0).start()

    total = part_ref[wa]
    for k in range(1, nwa):
        slot = lax.rem(wa + k, nwa)
        copy(slot, gz, k, 0).wait_recv()
        total = total + slots[slot]
    out_ref[...] = total

    @pl.when(lower)
    def _():
        more = None
        for k in range(nwa):
            copy(nwa + k, gz - 1, k, nwa).wait_recv()
            more = slots[nwa + k] if more is None else more + slots[nwa + k]
        out_ref[...] += more

    for k in range(1, nwa):
        copy(wa, gz, k, 0).wait_send()

    @pl.when(upper)
    def _():
        for k in range(nwa):
            copy(nwa + wa, gz + 1, k, nwa).wait_send()


def pair_values(squared):
    inverse = lax.rsqrt(squared)
    inverse = inverse * (1.5 - (0.5 * squared) * (inverse * inverse))
    distance = squared * inverse
    inverse2 = inverse * inverse
    t = 1.0 / (distance + 2.0)
    series = ERFC[6] * t + ERFC[5]
    for coeff in ERFC[4::-1]:
        series = series * t + coeff
    gauss = jnp.exp(-squared)
    screen = series * t * inverse
    near = inverse2 * (0.5 * radius * radius)
    iso = gauss * (screen * (0.75 + near) + half_gauss)
    dya = (gauss * inverse2) * (screen * (0.75 - 3.0 * near) + half_gauss)
    return iso, dya


def pairs_kernel(nall, nblocks, codes_ref, blocks_ref, out_ref, left, right, feats, acc, tiles, queue):
    rows_codes = codes_ref.shape[0]

    def push(step, count):
        for k in range(8):
            code = codes_ref[step * 8 + k]
            queue[count] = code
            count = count + jnp.where(code >= 0, 1, 0)
        return count

    count = lax.fori_loop(0, rows_codes // 8, push, jnp.int32(0))

    one = jnp.ones((1, BS), F32)
    zero = jnp.zeros((1, BS), F32)

    def prepare(block, carry):
        data = blocks_ref[block]
        x, f = data[0:3], data[3:6]
        high, mid, low = [p.astype(F32) for p in split3(x)]
        norm = jnp.sum(x * x, axis=0, keepdims=True)
        na = [p.astype(F32) for p in split3(norm + radius * radius)]
        nb = [p.astype(F32) for p in split3(norm)]
        left[block] = jnp.concatenate(
            [high, high, mid, high, low, mid, *na, one, one, one, *([zero] * 8)], axis=0
        ).astype(BF16)
        right[block] = jnp.concatenate(
            [-2.0 * p for p in (high, mid, high, low, high, mid)] + [one, one, one, *nb, *([zero] * 8)],
            axis=0,
        ).astype(BF16)
        along = jnp.sum(x * f, axis=0, keepdims=True)
        feat = jnp.concatenate(
            [f, along, f[0:1] * x, f[1:2] * x, f[2:3] * x, along * x], axis=0
        )
        fh, fl = split2(feat)
        feats[block] = jnp.concatenate([fh, fl], axis=0)
        acc[block] = jnp.zeros((24, BS), F32)
        return carry

    lax.fori_loop(0, nall, prepare, 0)

    def gather(block, weight, result_f, result_h):
        acc[block, 0:16] += weight * (result_h[0:16] + result_h[16:32])
        acc[block, 16:24] += weight * (result_f[0:8] + result_f[16:24])

    def pair(step, carry):
        code = queue[step]
        first, second = code // 4096, lax.rem(code, 4096)
        la, rb = left[first], right[second]
        for c in range(BS // CHUNK):
            rows = slice(c * CHUNK, (c + 1) * CHUNK)
            iso, dya = pair_values(dot(la[:, rows], rb, 0, 0))
            fh, fl = split2(iso)
            hh, hl = split2(dya)
            tiles[0, rows] = fh
            tiles[1, rows] = fl
            tiles[2, rows] = hh
            tiles[3, rows] = hl
        fa, fb = feats[first], feats[second]
        gather(
            first,
            1.0,
            dot(fb, tiles[0], 1, 1) + dot(fb, tiles[1], 1, 1),
            dot(fb, tiles[2], 1, 1) + dot(fb, tiles[3], 1, 1),
        )
        gather(
            second,
            jnp.where(first == second, 0.0, 1.0).astype(F32),
            dot(fa, tiles[0], 1, 0) + dot(fa, tiles[1], 1, 0),
            dot(fa, tiles[2], 1, 0) + dot(fa, tiles[3], 1, 0),
        )
        return carry

    lax.fori_loop(0, count, pair, 0)

    def finish(dev, carry):
        for k in range(nblocks):
            block = dev * nblocks + k
            x = blocks_ref[block, 0:3]
            a = acc[block]
            first = jnp.sum(x * a[0:3], axis=0, keepdims=True)
            second = x[0:1] * a[4:7] + x[1:2] * a[7:10] + x[2:3] * a[10:13]
            value = prefactor * (a[16:19] + (x * (first - a[3:4]) - (second - a[13:16])))
            out_ref[dev, k * ROWS : (k + 1) * ROWS] = jnp.concatenate(
                [value, jnp.zeros((ROWS - 3, BS), F32)], axis=0
            )
        return carry

    lax.fori_loop(0, nall // nblocks, finish, 0)


VMEM = pl.BlockSpec(memory_space=pltpu.VMEM)
SMEM = pl.BlockSpec(memory_space=pltpu.SMEM)
LIMIT = 48 * 1024 * 1024


def body(ngz, nwa, positions, forces, order, pair_list, pair_worker):
    per_dev = positions.shape[1]
    nblocks = per_dev // BS
    nall = 2 * nwa * nblocks
    listed = pair_worker.shape[0]
    order = order.reshape(1, per_dev)
    plain = pltpu.CompilerParams(vmem_limit_bytes=LIMIT)
    mine = pl.pallas_call(
        pick_kernel,
        out_shape=jax.ShapeDtypeStruct((nblocks, ROWS, BS), F32),
        in_specs=[VMEM] * 3,
        out_specs=VMEM,
        compiler_params=plain,
    )(positions, forces, order)
    blocks = pl.pallas_call(
        functools.partial(spread_kernel, ngz, nwa, nblocks),
        out_shape=jax.ShapeDtypeStruct((nall, ROWS, BS), F32),
        in_specs=[VMEM],
        out_specs=VMEM,
        scratch_shapes=[
            pltpu.SemaphoreType.DMA,
            pltpu.SemaphoreType.DMA((2 * nwa,)),
            pltpu.SemaphoreType.DMA((2 * nwa,)),
        ],
        compiler_params=pltpu.CompilerParams(
            collective_id=0, has_side_effects=True, vmem_limit_bytes=LIMIT
        ),
    )(mine)
    codes = jnp.where(
        pair_worker == lax.axis_index("wa"), pair_list[:, 0] * 4096 + pair_list[:, 1], -1
    )
    parts = pl.pallas_call(
        functools.partial(pairs_kernel, nall, nblocks),
        out_shape=jax.ShapeDtypeStruct((2 * nwa, nblocks * ROWS, BS), F32),
        in_specs=[SMEM, VMEM],
        out_specs=VMEM,
        scratch_shapes=[
            pltpu.VMEM((nall, 32, BS), BF16),
            pltpu.VMEM((nall, 32, BS), BF16),
            pltpu.VMEM((nall, 32, BS), BF16),
            pltpu.VMEM((nall, 24, BS), F32),
            pltpu.VMEM((4, BS, BS), BF16),
            pltpu.SMEM((listed + 8,), jnp.int32),
        ],
        compiler_params=plain,
    )(codes, blocks)
    owned = pl.pallas_call(
        functools.partial(collect_kernel, ngz, nwa),
        out_shape=jax.ShapeDtypeStruct((nblocks * ROWS, BS), F32),
        in_specs=[VMEM],
        out_specs=VMEM,
        scratch_shapes=[
            pltpu.VMEM((2 * nwa, nblocks * ROWS, BS), F32),
            pltpu.SemaphoreType.DMA((2 * nwa,)),
            pltpu.SemaphoreType.DMA((2 * nwa,)),
        ],
        compiler_params=pltpu.CompilerParams(
            collective_id=1, has_side_effects=True, vmem_limit_bytes=LIMIT
        ),
    )(parts)
    return pl.pallas_call(
        put_kernel,
        out_shape=jax.ShapeDtypeStruct((3, per_dev), F32),
        in_specs=[VMEM] * 2,
        out_specs=VMEM,
        compiler_params=plain,
    )(owned, order)


def solution(mesh):
    return jax.shard_map(
        functools.partial(body, mesh.shape["gz"], mesh.shape["wa"]),
        mesh=mesh,
        in_specs=(
            P(None, ("gz", "wa")),
            P(None, ("gz", "wa")),
            P(("gz", "wa")),
            P("gz", None),
            P("gz"),
        ),
        out_specs=P(None, ("gz", "wa")),
        check_vma=False,
    )
```

```python
import functools
import math

import jax
import jax.numpy as jnp
from jax import lax
from jax.experimental import pallas as pl
from jax.experimental.pallas import tpu as pltpu
from jax.sharding import PartitionSpec as P

BS = 256
ROWS = 8
SENT = 6
BACK = 16
CHUNK = 64

radius = 0.25
prefactor = 1.0 / (4.0 * math.pi)
half_gauss = 0.5 / math.sqrt(math.pi)
MESH = pl.DeviceIdType.MESH
F32 = jnp.float32
BF16 = jnp.bfloat16

ERFC = (0.565205955, 1.09670851, 2.38765618, -0.0810194158, 14.3292365, -25.4472659, 12.7559653)


def split2(value):
    high = value.astype(BF16)
    return high, (value - high.astype(F32)).astype(BF16)


def split3(value):
    high = value.astype(BF16)
    rest = value - high.astype(F32)
    mid = rest.astype(BF16)
    return high, mid, (rest - mid.astype(F32)).astype(BF16)


def dot(a, b, ca, cb):
    return lax.dot_general(a, b, (((ca,), (cb,)), ((), ())), preferred_element_type=F32)


def pick_kernel(pos_ref, force_ref, order_ref, out_ref):
    per_dev = pos_ref.shape[1]
    pad = jnp.zeros((2, per_dev), F32)
    parts = jnp.concatenate([pos_ref[...], force_ref[...], pad], axis=0)
    parts = jnp.concatenate([p.astype(F32) for p in split3(parts)], axis=0).astype(BF16)
    source = lax.broadcasted_iota(jnp.int32, (per_dev, BS), 0)
    for block in range(per_dev // BS):
        wanted = order_ref[:, block * BS : (block + 1) * BS]
        hot = jnp.where(source == wanted, 1.0, 0.0).astype(BF16)
        got = dot(parts, hot, 1, 0)
        got = (got[0:ROWS] + got[ROWS : 2 * ROWS]) + got[2 * ROWS : 3 * ROWS]
        out_ref[block * SENT : (block + 1) * SENT] = got[0:SENT]


def put_kernel(value_ref, order_ref, out_ref):
    per_dev = out_ref.shape[1]
    nblocks = per_dev // BS
    source = lax.broadcasted_iota(jnp.int32, (per_dev, BS), 0)
    total = None
    for block in range(nblocks):
        value = jnp.concatenate(
            [value_ref[3 * block : 3 * block + 3], jnp.zeros((ROWS - 3, BS), F32)], axis=0
        )
        parts = jnp.concatenate([p.astype(F32) for p in split3(value)], axis=0).astype(BF16)
        wanted = order_ref[:, block * BS : (block + 1) * BS]
        hot = jnp.where(source == wanted, 1.0, 0.0).astype(BF16)
        got = dot(parts, hot, 1, 1)
        total = got if total is None else total + got
    total = (total[0:ROWS] + total[ROWS : 2 * ROWS]) + total[2 * ROWS : 3 * ROWS]
    out_ref[...] = total[:3]


def spread_kernel(ngz, nwa, mine_ref, out_ref, local_sem, send_sem, recv_sem):
    gz, wa = lax.axis_index("gz"), lax.axis_index("wa")
    lower, upper = gz > 0, gz < ngz - 1
    barrier = pltpu.get_barrier_semaphore()
    for k in range(1, nwa):
        pl.semaphore_signal(barrier, inc=1, device_id=(gz, lax.rem(wa + k, nwa)), device_id_type=MESH)

    @pl.when(upper)
    def _():
        pl.semaphore_signal(barrier, inc=1, device_id=(gz + 1, wa), device_id_type=MESH)

    own = pltpu.make_async_copy(mine_ref, out_ref.at[wa], local_sem)
    own.start()
    pl.semaphore_wait(barrier, nwa - 1 + jnp.where(lower, 1, 0))

    def across(slot, k):
        return pltpu.make_async_remote_copy(
            src_ref=mine_ref,
            dst_ref=out_ref.at[slot],
            send_sem=send_sem.at[k],
            recv_sem=recv_sem.at[slot],
            device_id=(gz, lax.rem(wa + k, nwa)),
            device_id_type=MESH,
        )

    def down(k, to_gz):
        slot = lax.rem(wa + k, nwa)
        return pltpu.make_async_remote_copy(
            src_ref=mine_ref if k == 0 else out_ref.at[slot],
            dst_ref=out_ref.at[nwa + slot],
            send_sem=send_sem.at[nwa + k],
            recv_sem=recv_sem.at[nwa + slot],
            device_id=(to_gz, wa),
            device_id_type=MESH,
        )

    for k in range(1, nwa):
        across(wa, k).start()

    @pl.when(lower)
    def _():
        down(0, gz - 1).start()

    own.wait()
    for k in range(1, nwa):
        across(lax.rem(wa + k, nwa), k).wait_recv()

        @pl.when(lower)
        def _():
            down(k, gz - 1).start()

    @pl.when(upper)
    def _():
        for k in range(nwa):
            down(k, gz + 1).wait_recv()

    @pl.when(jnp.logical_not(upper))
    def _():
        out_ref[nwa:] = jnp.zeros((nwa,) + mine_ref.shape, F32)

    for k in range(1, nwa):
        across(wa, k).wait_send()

    @pl.when(lower)
    def _():
        for k in range(nwa):
            down(k, gz - 1).wait_send()


def collect_kernel(ngz, nwa, part_ref, out_ref, slots, send_sem, recv_sem):
    gz, wa = lax.axis_index("gz"), lax.axis_index("wa")
    lower, upper = gz > 0, gz < ngz - 1
    barrier = pltpu.get_barrier_semaphore()
    for k in range(1, nwa):
        pl.semaphore_signal(barrier, inc=1, device_id=(gz, lax.rem(wa + k, nwa)), device_id_type=MESH)

    @pl.when(lower)
    def _():
        for k in range(nwa):
            pl.semaphore_signal(barrier, inc=1, device_id=(gz - 1, lax.rem(wa + k, nwa)), device_id_type=MESH)

    pl.semaphore_wait(barrier, nwa - 1 + jnp.where(upper, nwa, 0))

    def copy(slot, to_gz, k, base):
        to = lax.rem(wa + k, nwa)
        return pltpu.make_async_remote_copy(
            src_ref=part_ref.at[base + to],
            dst_ref=slots.at[slot],
            send_sem=send_sem.at[base + k],
            recv_sem=recv_sem.at[slot],
            device_id=(to_gz, to),
            device_id_type=MESH,
        )

    @pl.when(upper)
    def _():
        for k in range(nwa):
            copy(nwa + wa, gz + 1, k, nwa).start()

    for k in range(1, nwa):
        copy(wa, gz, k, 0).start()

    total = part_ref[wa]
    for k in range(1, nwa):
        slot = lax.rem(wa + k, nwa)
        copy(slot, gz, k, 0).wait_recv()
        total = total + slots[slot]
    out_ref[...] = total

    @pl.when(lower)
    def _():
        more = None
        for k in range(nwa):
            copy(nwa + k, gz - 1, k, nwa).wait_recv()
            more = slots[nwa + k] if more is None else more + slots[nwa + k]
        out_ref[...] += more

    for k in range(1, nwa):
        copy(wa, gz, k, 0).wait_send()

    @pl.when(upper)
    def _():
        for k in range(nwa):
            copy(nwa + wa, gz + 1, k, nwa).wait_send()


def pair_values(squared):
    inverse = lax.rsqrt(squared)
    distance = squared * inverse
    inverse2 = inverse * inverse
    shifted = distance + 2.0
    t = pl.reciprocal(shifted, approx=True)
    t = t * (2.0 - shifted * t)
    series = ERFC[6] * t + ERFC[5]
    for coeff in ERFC[4::-1]:
        series = series * t + coeff
    gauss = jnp.exp2(squared * (-1.0 / math.log(2.0)))
    screen = series * (t * inverse)
    near = (screen * inverse2) * (0.5 * radius * radius)
    far = 0.75 * screen + half_gauss
    iso = gauss * (far + near)
    dya = (gauss * inverse2) * (far - 3.0 * near)
    return iso, dya


def pairs_kernel(nall, nblocks, codes_ref, blocks_ref, out_ref, left, right, feats, acc, tiles, tiles_b, queue):
    rows_codes = codes_ref.shape[0]

    def push(step, count):
        for k in range(8):
            code = codes_ref[step * 8 + k]
            queue[count] = code
            count = count + jnp.where(code >= 0, 1, 0)
        return count

    count = lax.fori_loop(0, rows_codes // 8, push, jnp.int32(0))

    one = jnp.ones((1, BS), F32)
    zero = jnp.zeros((1, BS), F32)

    def prepare_all(dev, carry):
        for k in range(nblocks):
            data = blocks_ref[dev, k * SENT : (k + 1) * SENT]
            prepare(dev * nblocks + k, data[0:3], data[3:6])
        return carry

    def prepare(block, x, f):
        high, mid, low = [p.astype(F32) for p in split3(x)]
        norm = jnp.sum(x * x, axis=0, keepdims=True)
        na = [p.astype(F32) for p in split3(norm + radius * radius)]
        nb = [p.astype(F32) for p in split3(norm)]
        left[block] = jnp.concatenate(
            [high, high, mid, high, low, mid, *na, one, one, one, *([zero] * 8)], axis=0
        ).astype(BF16)
        right[block] = jnp.concatenate(
            [-2.0 * p for p in (high, mid, high, low, high, mid)] + [one, one, one, *nb, *([zero] * 8)],
            axis=0,
        ).astype(BF16)
        along = jnp.sum(x * f, axis=0, keepdims=True)
        feat = jnp.concatenate(
            [f, along, f[0:1] * x, f[1:2] * x, f[2:3] * x, along * x], axis=0
        )
        fh, fl = split2(feat)
        feats[block] = jnp.concatenate([fh, fl], axis=0)
        acc[block] = jnp.zeros((24, BS), F32)

    lax.fori_loop(0, nall // nblocks, prepare_all, 0)

    def gather(block, weight, result_f, result_h):
        acc[block, 0:16] += weight * (result_h[0:16] + result_h[16:32])
        acc[block, 16:24] += weight * (result_f[0:8] + result_f[16:24])

    def evaluate(step, into):
        code = queue[step]
        la, rb = left[code // 4096], right[lax.rem(code, 4096)]
        for c in range(BS // CHUNK):
            rows = slice(c * CHUNK, (c + 1) * CHUNK)
            iso, dya = pair_values(dot(la[:, rows], rb, 0, 0))
            fh, fl = split2(iso)
            hh, hl = split2(dya)
            into[0, rows] = fh
            into[1, rows] = fl
            into[2, rows] = hh
            into[3, rows] = hl

    def apply(step, held):
        live = jnp.logical_and(step >= 0, step < count)
        code = queue[jnp.maximum(step, 0)]
        first, second = code // 4096, lax.rem(code, 4096)
        fa, fb = feats[first], feats[second]
        both = jnp.logical_and(live, first != second)
        gather(
            first,
            jnp.where(live, 1.0, 0.0).astype(F32),
            dot(fb, held[0], 1, 1) + dot(fb, held[1], 1, 1),
            dot(fb, held[2], 1, 1) + dot(fb, held[3], 1, 1),
        )
        gather(
            second,
            jnp.where(both, 1.0, 0.0).astype(F32),
            dot(fa, held[0], 1, 0) + dot(fa, held[1], 1, 0),
            dot(fa, held[2], 1, 0) + dot(fa, held[3], 1, 0),
        )

    queue[count] = 0
    tiles_b[...] = jnp.zeros((4, BS, BS), BF16)

    def two(step, carry):
        evaluate(2 * step, tiles)
        apply(2 * step - 1, tiles_b)
        evaluate(2 * step + 1, tiles_b)
        apply(2 * step, tiles)
        return carry

    steps = (count + 1) // 2
    lax.fori_loop(0, steps, two, 0)
    apply(2 * steps - 1, tiles_b)

    def finish(dev, carry):
        values = []
        for k in range(nblocks):
            x = blocks_ref[dev, k * SENT : k * SENT + 3]
            a = acc[dev * nblocks + k]
            first = jnp.sum(x * a[0:3], axis=0, keepdims=True)
            second = x[0:1] * a[4:7] + x[1:2] * a[7:10] + x[2:3] * a[10:13]
            values.append(prefactor * (a[16:19] + (x * (first - a[3:4]) - (second - a[13:16]))))
        values.append(jnp.zeros((BACK - 3 * nblocks, BS), F32))
        out_ref[dev] = jnp.concatenate(values, axis=0)
        return carry

    lax.fori_loop(0, nall // nblocks, finish, 0)


VMEM = pl.BlockSpec(memory_space=pltpu.VMEM)
SMEM = pl.BlockSpec(memory_space=pltpu.SMEM)
LIMIT = 48 * 1024 * 1024


def body(ngz, nwa, positions, forces, order, pair_list, pair_worker):
    per_dev = positions.shape[1]
    nblocks = per_dev // BS
    nall = 2 * nwa * nblocks
    listed = pair_worker.shape[0]
    order = order.reshape(1, per_dev)
    plain = pltpu.CompilerParams(vmem_limit_bytes=LIMIT)
    mine = pl.pallas_call(
        pick_kernel,
        out_shape=jax.ShapeDtypeStruct((nblocks * SENT, BS), F32),
        in_specs=[VMEM] * 3,
        out_specs=VMEM,
        compiler_params=plain,
    )(positions, forces, order)
    blocks = pl.pallas_call(
        functools.partial(spread_kernel, ngz, nwa),
        out_shape=jax.ShapeDtypeStruct((2 * nwa, nblocks * SENT, BS), F32),
        in_specs=[VMEM],
        out_specs=VMEM,
        scratch_shapes=[
            pltpu.SemaphoreType.DMA,
            pltpu.SemaphoreType.DMA((2 * nwa,)),
            pltpu.SemaphoreType.DMA((2 * nwa,)),
        ],
        compiler_params=pltpu.CompilerParams(
            collective_id=0, has_side_effects=True, vmem_limit_bytes=LIMIT
        ),
    )(mine)
    codes = jnp.where(
        pair_worker == lax.axis_index("wa"), pair_list[:, 0] * 4096 + pair_list[:, 1], -1
    )
    parts = pl.pallas_call(
        functools.partial(pairs_kernel, nall, nblocks),
        out_shape=jax.ShapeDtypeStruct((2 * nwa, BACK, BS), F32),
        in_specs=[SMEM, VMEM],
        out_specs=VMEM,
        scratch_shapes=[
            pltpu.VMEM((nall, 32, BS), BF16),
            pltpu.VMEM((nall, 32, BS), BF16),
            pltpu.VMEM((nall, 32, BS), BF16),
            pltpu.VMEM((nall, 24, BS), F32),
            pltpu.VMEM((4, BS, BS), BF16),
            pltpu.VMEM((4, BS, BS), BF16),
            pltpu.SMEM((listed + 8,), jnp.int32),
        ],
        compiler_params=plain,
    )(codes, blocks)
    owned = pl.pallas_call(
        functools.partial(collect_kernel, ngz, nwa),
        out_shape=jax.ShapeDtypeStruct((BACK, BS), F32),
        in_specs=[VMEM],
        out_specs=VMEM,
        scratch_shapes=[
            pltpu.VMEM((2 * nwa, BACK, BS), F32),
            pltpu.SemaphoreType.DMA((2 * nwa,)),
            pltpu.SemaphoreType.DMA((2 * nwa,)),
        ],
        compiler_params=pltpu.CompilerParams(
            collective_id=1, has_side_effects=True, vmem_limit_bytes=LIMIT
        ),
    )(parts)
    return pl.pallas_call(
        put_kernel,
        out_shape=jax.ShapeDtypeStruct((3, per_dev), F32),
        in_specs=[VMEM] * 2,
        out_specs=VMEM,
        compiler_params=plain,
    )(owned, order)


def solution(mesh):
    return jax.shard_map(
        functools.partial(body, mesh.shape["gz"], mesh.shape["wa"]),
        mesh=mesh,
        in_specs=(
            P(None, ("gz", "wa")),
            P(None, ("gz", "wa")),
            P(("gz", "wa")),
            P("gz", None),
            P("gz"),
        ),
        out_specs=P(None, ("gz", "wa")),
        check_vma=False,
    )
```

```python
import functools
import math

import jax
import jax.numpy as jnp
from jax import lax
from jax.experimental import pallas as pl
from jax.experimental.pallas import tpu as pltpu
from jax.sharding import PartitionSpec as P

BS = 256
ROWS = 8
SENT = 6
BACK = 16
CHUNK = 64

radius = 0.25
prefactor = 1.0 / (4.0 * math.pi)
half_gauss = 0.5 / math.sqrt(math.pi)
MESH = pl.DeviceIdType.MESH
F32 = jnp.float32
BF16 = jnp.bfloat16

ERFC = (0.565205955, 1.09670851, 2.38765618, -0.0810194158, 14.3292365, -25.4472659, 12.7559653)


def split2(value):
    high = value.astype(BF16)
    return high, (value - high.astype(F32)).astype(BF16)


def split3(value):
    high = value.astype(BF16)
    rest = value - high.astype(F32)
    mid = rest.astype(BF16)
    return high, mid, (rest - mid.astype(F32)).astype(BF16)


def dot(a, b, ca, cb):
    return lax.dot_general(a, b, (((ca,), (cb,)), ((), ())), preferred_element_type=F32)


def pick_kernel(*refs):
    sources, (out_ref, codes_ref), held, sems = refs[:5], refs[5:7], refs[7:12], refs[12]
    copies = [pltpu.make_async_copy(a, b, sems.at[k]) for k, (a, b) in enumerate(zip(sources, held))]
    for copy in copies:
        copy.start()
    for copy in copies:
        copy.wait()
    pos_ref, force_ref, order_ref, list_ref, worker_ref = held
    codes_ref[...] = jnp.where(
        worker_ref[...] == lax.axis_index("wa"), list_ref[0:1] * 4096 + list_ref[1:2], -1
    )
    per_dev = pos_ref.shape[1]
    pad = jnp.zeros((2, per_dev), F32)
    parts = jnp.concatenate([pos_ref[...], force_ref[...], pad], axis=0)
    parts = jnp.concatenate([p.astype(F32) for p in split3(parts)], axis=0).astype(BF16)
    source = lax.broadcasted_iota(jnp.int32, (per_dev, BS), 0)
    for block in range(per_dev // BS):
        wanted = order_ref[:, block * BS : (block + 1) * BS]
        hot = jnp.where(source == wanted, 1.0, 0.0).astype(BF16)
        got = dot(parts, hot, 1, 0)
        got = (got[0:ROWS] + got[ROWS : 2 * ROWS]) + got[2 * ROWS : 3 * ROWS]
        out_ref[block * SENT : (block + 1) * SENT] = got[0:SENT]


def put_kernel(value_ref, order_ref, out_ref):
    per_dev = out_ref.shape[1]
    nblocks = per_dev // BS
    source = lax.broadcasted_iota(jnp.int32, (per_dev, BS), 0)
    total = None
    for block in range(nblocks):
        value = jnp.concatenate(
            [value_ref[3 * block : 3 * block + 3], jnp.zeros((ROWS - 3, BS), F32)], axis=0
        )
        parts = jnp.concatenate([p.astype(F32) for p in split3(value)], axis=0).astype(BF16)
        wanted = order_ref[:, block * BS : (block + 1) * BS]
        hot = jnp.where(source == wanted, 1.0, 0.0).astype(BF16)
        got = dot(parts, hot, 1, 1)
        total = got if total is None else total + got
    total = (total[0:ROWS] + total[ROWS : 2 * ROWS]) + total[2 * ROWS : 3 * ROWS]
    out_ref[...] = total[:3]


def spread_kernel(ngz, nwa, mine_ref, out_ref, local_sem, send_sem, recv_sem):
    gz, wa = lax.axis_index("gz"), lax.axis_index("wa")
    lower, upper = gz > 0, gz < ngz - 1
    barrier = pltpu.get_barrier_semaphore()
    for k in range(1, nwa):
        pl.semaphore_signal(barrier, inc=1, device_id=(gz, lax.rem(wa + k, nwa)), device_id_type=MESH)

    @pl.when(upper)
    def _():
        pl.semaphore_signal(barrier, inc=1, device_id=(gz + 1, wa), device_id_type=MESH)

    own = pltpu.make_async_copy(mine_ref, out_ref.at[wa], local_sem)
    own.start()
    pl.semaphore_wait(barrier, nwa - 1 + jnp.where(lower, 1, 0))

    def across(slot, k):
        return pltpu.make_async_remote_copy(
            src_ref=mine_ref,
            dst_ref=out_ref.at[slot],
            send_sem=send_sem.at[k],
            recv_sem=recv_sem.at[slot],
            device_id=(gz, lax.rem(wa + k, nwa)),
            device_id_type=MESH,
        )

    def down(k, to_gz):
        slot = lax.rem(wa + k, nwa)
        return pltpu.make_async_remote_copy(
            src_ref=mine_ref if k == 0 else out_ref.at[slot],
            dst_ref=out_ref.at[nwa + slot],
            send_sem=send_sem.at[nwa + k],
            recv_sem=recv_sem.at[nwa + slot],
            device_id=(to_gz, wa),
            device_id_type=MESH,
        )

    for k in range(1, nwa):
        across(wa, k).start()

    @pl.when(lower)
    def _():
        down(0, gz - 1).start()

    own.wait()
    for k in range(1, nwa):
        across(lax.rem(wa + k, nwa), k).wait_recv()

        @pl.when(lower)
        def _():
            down(k, gz - 1).start()

    @pl.when(upper)
    def _():
        for k in range(nwa):
            down(k, gz + 1).wait_recv()

    @pl.when(jnp.logical_not(upper))
    def _():
        out_ref[nwa:] = jnp.zeros((nwa,) + mine_ref.shape, F32)

    for k in range(1, nwa):
        across(wa, k).wait_send()

    @pl.when(lower)
    def _():
        for k in range(nwa):
            down(k, gz - 1).wait_send()


def collect_kernel(ngz, nwa, part_ref, out_ref, slots, send_sem, recv_sem):
    gz, wa = lax.axis_index("gz"), lax.axis_index("wa")
    lower, upper = gz > 0, gz < ngz - 1
    barrier = pltpu.get_barrier_semaphore()
    for k in range(1, nwa):
        pl.semaphore_signal(barrier, inc=1, device_id=(gz, lax.rem(wa + k, nwa)), device_id_type=MESH)

    @pl.when(lower)
    def _():
        for k in range(nwa):
            pl.semaphore_signal(barrier, inc=1, device_id=(gz - 1, lax.rem(wa + k, nwa)), device_id_type=MESH)

    pl.semaphore_wait(barrier, nwa - 1 + jnp.where(upper, nwa, 0))

    def copy(slot, to_gz, k, base):
        to = lax.rem(wa + k, nwa)
        return pltpu.make_async_remote_copy(
            src_ref=part_ref.at[base + to],
            dst_ref=slots.at[slot],
            send_sem=send_sem.at[base + k],
            recv_sem=recv_sem.at[slot],
            device_id=(to_gz, to),
            device_id_type=MESH,
        )

    @pl.when(upper)
    def _():
        for k in range(nwa):
            copy(nwa + wa, gz + 1, k, nwa).start()

    for k in range(1, nwa):
        copy(wa, gz, k, 0).start()

    total = part_ref[wa]
    for k in range(1, nwa):
        slot = lax.rem(wa + k, nwa)
        copy(slot, gz, k, 0).wait_recv()
        total = total + slots[slot]
    out_ref[...] = total

    @pl.when(lower)
    def _():
        more = None
        for k in range(nwa):
            copy(nwa + k, gz - 1, k, nwa).wait_recv()
            more = slots[nwa + k] if more is None else more + slots[nwa + k]
        out_ref[...] += more

    for k in range(1, nwa):
        copy(wa, gz, k, 0).wait_send()

    @pl.when(upper)
    def _():
        for k in range(nwa):
            copy(nwa + wa, gz + 1, k, nwa).wait_send()


def pair_values(squared):
    inverse = lax.rsqrt(squared)
    distance = squared * inverse
    inverse2 = inverse * inverse
    shifted = distance + 2.0
    t = pl.reciprocal(shifted, approx=True)
    t = t * (2.0 - shifted * t)
    series = ERFC[6] * t + ERFC[5]
    for coeff in ERFC[4::-1]:
        series = series * t + coeff
    gauss = jnp.exp2(squared * (-1.0 / math.log(2.0)))
    screen = series * (t * inverse)
    near = (screen * inverse2) * (0.5 * radius * radius)
    far = 0.75 * screen + half_gauss
    iso = gauss * (far + near)
    dya = (gauss * inverse2) * (far - 3.0 * near)
    return iso, dya


def pairs_kernel(nall, nblocks, codes_ref, blocks_ref, out_ref, left, right, feats, acc, tiles, tiles_b, queue):
    rows_codes = codes_ref.shape[1]

    def push(step, count):
        for k in range(8):
            code = codes_ref[0, step * 8 + k]
            queue[count] = code
            count = count + jnp.where(code >= 0, 1, 0)
        return count

    count = lax.fori_loop(0, rows_codes // 8, push, jnp.int32(0))

    one = jnp.ones((1, BS), F32)
    zero = jnp.zeros((1, BS), F32)

    def prepare_all(dev, carry):
        for k in range(nblocks):
            data = blocks_ref[dev, k * SENT : (k + 1) * SENT]
            prepare(dev * nblocks + k, data[0:3], data[3:6])
        return carry

    def prepare(block, x, f):
        high, mid, low = [p.astype(F32) for p in split3(x)]
        norm = jnp.sum(x * x, axis=0, keepdims=True)
        na = [p.astype(F32) for p in split3(norm + radius * radius)]
        nb = [p.astype(F32) for p in split3(norm)]
        left[block] = jnp.concatenate(
            [high, high, mid, high, low, mid, *na, one, one, one, *([zero] * 8)], axis=0
        ).astype(BF16)
        right[block] = jnp.concatenate(
            [-2.0 * p for p in (high, mid, high, low, high, mid)] + [one, one, one, *nb, *([zero] * 8)],
            axis=0,
        ).astype(BF16)
        along = jnp.sum(x * f, axis=0, keepdims=True)
        feat = jnp.concatenate(
            [f, along, f[0:1] * x, f[1:2] * x, f[2:3] * x, along * x], axis=0
        )
        fh, fl = split2(feat)
        feats[block] = jnp.concatenate([fh, fl], axis=0)
        acc[block] = jnp.zeros((24, BS), F32)

    lax.fori_loop(0, nall // nblocks, prepare_all, 0)

    def gather(block, weight, result_f, result_h):
        acc[block, 0:16] += weight * (result_h[0:16] + result_h[16:32])
        acc[block, 16:24] += weight * (result_f[0:8] + result_f[16:24])

    def evaluate(step, into):
        code = queue[step]
        la, rb = left[code // 4096], right[lax.rem(code, 4096)]
        for c in range(BS // CHUNK):
            rows = slice(c * CHUNK, (c + 1) * CHUNK)
            iso, dya = pair_values(dot(la[:, rows], rb, 0, 0))
            fh, fl = split2(iso)
            hh, hl = split2(dya)
            into[0, rows] = fh
            into[1, rows] = fl
            into[2, rows] = hh
            into[3, rows] = hl

    def apply(step, held):
        live = jnp.logical_and(step >= 0, step < count)
        code = queue[jnp.maximum(step, 0)]
        first, second = code // 4096, lax.rem(code, 4096)
        fa, fb = feats[first], feats[second]
        both = jnp.logical_and(live, first != second)
        gather(
            first,
            jnp.where(live, 1.0, 0.0).astype(F32),
            dot(fb, held[0], 1, 1) + dot(fb, held[1], 1, 1),
            dot(fb, held[2], 1, 1) + dot(fb, held[3], 1, 1),
        )
        gather(
            second,
            jnp.where(both, 1.0, 0.0).astype(F32),
            dot(fa, held[0], 1, 0) + dot(fa, held[1], 1, 0),
            dot(fa, held[2], 1, 0) + dot(fa, held[3], 1, 0),
        )

    queue[count] = 0
    tiles_b[...] = jnp.zeros((4, BS, BS), BF16)

    def two(step, carry):
        evaluate(2 * step, tiles)
        apply(2 * step - 1, tiles_b)
        evaluate(2 * step + 1, tiles_b)
        apply(2 * step, tiles)
        return carry

    steps = (count + 1) // 2
    lax.fori_loop(0, steps, two, 0)
    apply(2 * steps - 1, tiles_b)

    def finish(dev, carry):
        values = []
        for k in range(nblocks):
            x = blocks_ref[dev, k * SENT : k * SENT + 3]
            a = acc[dev * nblocks + k]
            first = jnp.sum(x * a[0:3], axis=0, keepdims=True)
            second = x[0:1] * a[4:7] + x[1:2] * a[7:10] + x[2:3] * a[10:13]
            values.append(prefactor * (a[16:19] + (x * (first - a[3:4]) - (second - a[13:16]))))
        values.append(jnp.zeros((BACK - 3 * nblocks, BS), F32))
        out_ref[dev] = jnp.concatenate(values, axis=0)
        return carry

    lax.fori_loop(0, nall // nblocks, finish, 0)


VMEM = pl.BlockSpec(memory_space=pltpu.VMEM)
SMEM = pl.BlockSpec(memory_space=pltpu.SMEM)
LIMIT = 48 * 1024 * 1024


def body(ngz, nwa, positions, forces, order, pair_list, pair_worker):
    per_dev = positions.shape[1]
    nblocks = per_dev // BS
    nall = 2 * nwa * nblocks
    listed = pair_worker.shape[0]
    order = order.reshape(1, per_dev)
    plain = pltpu.CompilerParams(vmem_limit_bytes=LIMIT)
    mine, codes = pl.pallas_call(
        pick_kernel,
        out_shape=(
            jax.ShapeDtypeStruct((nblocks * SENT, BS), F32),
            jax.ShapeDtypeStruct((1, listed), jnp.int32),
        ),
        in_specs=[pl.BlockSpec(memory_space=pl.ANY)] * 5,
        out_specs=(VMEM, VMEM),
        scratch_shapes=[
            pltpu.VMEM((3, per_dev), F32),
            pltpu.VMEM((3, per_dev), F32),
            pltpu.VMEM((1, per_dev), jnp.int32),
            pltpu.VMEM((2, listed), jnp.int32),
            pltpu.VMEM((1, listed), jnp.int32),
            pltpu.SemaphoreType.DMA((5,)),
        ],
        compiler_params=plain,
    )(positions, forces, order, pair_list.T, pair_worker.reshape(1, listed))
    blocks = pl.pallas_call(
        functools.partial(spread_kernel, ngz, nwa),
        out_shape=jax.ShapeDtypeStruct((2 * nwa, nblocks * SENT, BS), F32),
        in_specs=[VMEM],
        out_specs=VMEM,
        scratch_shapes=[
            pltpu.SemaphoreType.DMA,
            pltpu.SemaphoreType.DMA((2 * nwa,)),
            pltpu.SemaphoreType.DMA((2 * nwa,)),
        ],
        compiler_params=pltpu.CompilerParams(
            collective_id=0, has_side_effects=True, vmem_limit_bytes=LIMIT
        ),
    )(mine)
    parts = pl.pallas_call(
        functools.partial(pairs_kernel, nall, nblocks),
        out_shape=jax.ShapeDtypeStruct((2 * nwa, BACK, BS), F32),
        in_specs=[SMEM, VMEM],
        out_specs=VMEM,
        scratch_shapes=[
            pltpu.VMEM((nall, 32, BS), BF16),
            pltpu.VMEM((nall, 32, BS), BF16),
            pltpu.VMEM((nall, 32, BS), BF16),
            pltpu.VMEM((nall, 24, BS), F32),
            pltpu.VMEM((4, BS, BS), BF16),
            pltpu.VMEM((4, BS, BS), BF16),
            pltpu.SMEM((listed + 8,), jnp.int32),
        ],
        compiler_params=plain,
    )(codes, blocks)
    owned = pl.pallas_call(
        functools.partial(collect_kernel, ngz, nwa),
        out_shape=jax.ShapeDtypeStruct((BACK, BS), F32),
        in_specs=[VMEM],
        out_specs=VMEM,
        scratch_shapes=[
            pltpu.VMEM((2 * nwa, BACK, BS), F32),
            pltpu.SemaphoreType.DMA((2 * nwa,)),
            pltpu.SemaphoreType.DMA((2 * nwa,)),
        ],
        compiler_params=pltpu.CompilerParams(
            collective_id=1, has_side_effects=True, vmem_limit_bytes=LIMIT
        ),
    )(parts)
    return pl.pallas_call(
        put_kernel,
        out_shape=jax.ShapeDtypeStruct((3, per_dev), F32),
        in_specs=[VMEM] * 2,
        out_specs=VMEM,
        compiler_params=plain,
    )(owned, order)


def solution(mesh):
    return jax.shard_map(
        functools.partial(body, mesh.shape["gz"], mesh.shape["wa"]),
        mesh=mesh,
        in_specs=(
            P(None, ("gz", "wa")),
            P(None, ("gz", "wa")),
            P(("gz", "wa")),
            P("gz", None),
            P("gz"),
        ),
        out_specs=P(None, ("gz", "wa")),
        check_vma=False,
    )
```
